256 devices in a mesh: section: 4 (over x_lo, core), seq: 2 (over x_hi), tensor: 32 (over y, z).
Axes of the slice: x: 4 (x_hi: 2, x_lo: 2; x = x_hi * 2 + x_lo), y: 4, z: 8, core: 2. Of those that a mesh axis runs over, the one named last changes fastest.
Arguments:
- grad_out: bfloat16 [6144, 8192], P(('section', 'seq', 'tensor')), parts along dimension 0, may hold values from -6 to 6
- gate_pre: bfloat16 [6144, 26624], P(('section', 'seq'), 'tensor'), parts along dimension 0, may hold values from -6 to 6
- up_pre: bfloat16 [6144, 26624], P(('section', 'seq'), 'tensor'), parts along dimension 0, may hold values from -6 to 6
- down_weight: bfloat16 [106496, 8192], P(('section', 'tensor'), 'seq'), parts along dimension 0, may hold values from -0.0625 to 0.0625
- live_rows: int32 [8], P('section'), parts along dimension 0, may hold values from 96 to 768, as said below
Outputs:
- gate_grad: bfloat16 [6144, 26624], P(('section', 'seq'), 'tensor'), parts along dimension 0
- up_grad: bfloat16 [6144, 26624], P(('section', 'seq'), 'tensor'), parts along dimension 0
The draws below stay inside these ranges and needn't reach their ends.
There are 4 independent parts, one for each index of `section`. The reference program is written for one: setup_inputs(seed, part) draws one part's arguments, and reference() takes and returns one part's arrays. A program takes and returns all parts, laid end to end along the dimension named above; each array names one. Nothing has to cross between parts.
Inputs may be any that keep to these rules, and one draw needn't show every extreme that they name: `live_rows`: in every draw one sequence shard is live in all its 768 rows; the others at least 96.
All inputs are finite; a program needn't handle non-finite values.
Results may differ from the reference program's by a relative error of at most 0.001.
Values may be sent and summed in bfloat16 or wider, within the bound.
A program may use at most 128 MiB of HBM per device.

```python
import jax
import jax.numpy as jnp
from jax import lax

D = 8192
TOK_SEQ = 768
FF = 26624
TOKENS = 1536
N_SEQ = 2


def draw_live_rows(key, part):
    key = jax.random.fold_in(key, 11)
    key_counts, key_shard = jax.random.split(key)
    counts = jax.random.randint(key_counts, (N_SEQ,), TOK_SEQ // 8, TOK_SEQ + 1)
    full_shard = jax.random.randint(key_shard, (), 0, N_SEQ)
    return jnp.where(jnp.arange(N_SEQ) == full_shard, TOK_SEQ, counts).astype(jnp.int32)


def steps_of(key, dims, cuts, smallest, largest):
    def one(dim, blocks):
        steps = jax.random.uniform(jax.random.fold_in(jax.random.fold_in(key, 6), dim), (blocks,), jnp.float32, smallest / len(cuts), largest / len(cuts))
        return jnp.repeat(jnp.exp(steps), dims[dim] // blocks).reshape((-1,) + (1,) * (len(dims) - dim - 1))

    factor_of = one(*cuts[0])
    for cut in cuts[1:]:
        factor_of = factor_of * one(*cut)
    return factor_of


def noise(own_key, dims, deviation, reach, shards=(), held_as=jnp.bfloat16):
    drawn = deviation * jax.random.normal(own_key, dims, jnp.float32)
    if shards:
        drawn = drawn * steps_of(own_key, dims, shards, -0.22, 0.18)
    return jnp.clip(drawn, -reach, reach).astype(held_as)


def setup_inputs(seed: int = 0, part: int = 0) -> dict:
    streams_of = jax.random.split(jax.random.key(seed), 6)
    part_splits = jax.random.split(jax.random.fold_in(streams_of[5], part), 6)
    return {
        "grad_out": noise(part_splits[0], (TOKENS, D), 1.0, 6.0, ((0, 64),)),
        "gate_pre": noise(part_splits[1], (TOKENS, FF), 1.5, 6.0, ((0, 2), (1, 32))),
        "up_pre": noise(part_splits[2], (TOKENS, FF), 1.0, 6.0, ((0, 2), (1, 32))),
        "down_weight": noise(part_splits[3], (FF, D), D ** -0.5, 0.0625, ((0, 32), (1, 2))),
        "live_rows": draw_live_rows(jax.random.fold_in(jax.random.fold_in(streams_of[5], part), 71), part),
    }


def reference(grad_out, gate_pre, up_pre, down_weight, live_rows):
    hidden_grad = lax.dot_general(grad_out, down_weight, (((1,), (1,)), ((), ())), preferred_element_type=jnp.float32)
    row_ids = jnp.arange(TOKENS, dtype=jnp.int32)
    shard_ids = row_ids // TOK_SEQ
    local_ids = row_ids - shard_ids * TOK_SEQ
    bounds = jnp.take(live_rows, shard_ids)
    live_mask = (local_ids < bounds).astype(jnp.float32)
    hidden_grad = hidden_grad * live_mask[:, None]
    gate_value = gate_pre.astype(jnp.float32)
    up_value = up_pre.astype(jnp.float32)
    sigmoid_gate = jax.nn.sigmoid(gate_value)
    up_grad = (hidden_grad * gate_value * sigmoid_gate).astype(jnp.bfloat16)
    gate_grad = (hidden_grad * up_value * sigmoid_gate * (1.0 + gate_value * (1.0 - sigmoid_gate))).astype(jnp.bfloat16)
    return gate_grad, up_grad
```

```python
import functools

import jax
import jax.numpy as jnp
from jax import lax
from jax.experimental import pallas as pl
from jax.experimental.pallas import tpu as pltpu
from jax.sharding import PartitionSpec as P

MESH = pl.DeviceIdType.MESH
NY, NZ = 4, 8
ROWS, FEATS, UNITS = 24, 4096, 832
CUT = 2560
PARTS = ((0, CUT), (CUT, FEATS - CUT))
STEP = 1024
Y_HOPS = (0, 1, 2, -1)
Z_HOPS = (0, 1, 2, 3, 4, -1, -2, -3)
OTHER, OWN = 0, 1
ORDER = (
    104, 120, 72, 88, 1, 5, 8, 24, 33, 37, 40, 56, 2, 6, 9, 25, 34, 38, 48, 29, 3, 7, 13, 26, 35, 39, 10, 4, 45,
    30, 14, 61, 36, 27, 46, 41, 11, 62, 31, -1, 57, 15, 47, 28, 42, 69, 12, 58, 16, 63, 43, 17, 93, 70, 59, 21,
    44, 53, 18, 60, 94, 71, 65, 22, 54, -1, 49, 19, 101, 95, -1, 66, 55, 23, 89, 102, 50, 20, 109, 90, 67, 112,
    103, 73, 125, 51, 77, 110, 91, 68, 126, 74, 52, 111, 78, 92, 97, 127, 75, -1, 98, 79, 117, 76, 105, 121, 80,
    118, 99, 81, 106, 85, 122, 119, 100, 82, 107, 86, 123, -1, 108, 83, 124, 87, 113, 84, -1, 114, -1, 115, 116,
    -1,
)
DEPTH = 1
NEEDS = ((0,), (1, -1), (), (2,))


def packet(code):
    return (code // 64, code // 32 % 2, Y_HOPS[code // 8 % 4], Z_HOPS[code % 8])


def before(hops):
    return hops - 1 if hops > 0 else hops + 1


def origin_of(code):
    whose, part, hy, hz = packet(code)
    along_y = hy != 0 if part == 0 else hz == 0
    if along_y:
        return (whose, part, before(hy), hz), (0, 1 if hy > 0 else -1)
    return (whose, part, hy, before(hz)), (1, 1 if hz > 0 else -1)


def slot_of(name):
    whose, part, hy, hz = name
    return (part, whose, Y_HOPS.index(hy) * NZ + Z_HOPS.index(hz))


def kernel(x_hbm, w_hbm, gate_hbm, up_hbm, live_ref, gate_out, up_out,
           rows, w, gate, up, acc, tiles, arrived, out_g, out_u,
           send_sem, recv_sem, x_send, x_recv, c_send, c_recv, load_sem, out_sem):
    section, q, t = lax.axis_index("section"), lax.axis_index("seq"), lax.axis_index("tensor")
    y, z = t // NZ, t % NZ
    way = 1 - 2 * (section % 2)
    half = y % 2
    partner = (section, 1 - q, t)
    source = (q, 1 - q)

    def neighbour(link):
        axis, sign = link
        step = sign * way
        if axis == 0:
            return (section, q, (y + step + NY) % NY * NZ + z)
        return (section, q, y * NZ + (z + step + NZ) % NZ)

    def region(name):
        whose, part, hy, hz = name
        start, width = PARTS[part]
        shard = q if whose == OWN else 1 - q
        from_y = (y - way * hy + NY) % NY
        from_z = (z - way * hz + NZ) % NZ
        return rows.at[shard, from_y, from_z, :, pl.ds(start, width)]

    def sending(code):
        name, link = origin_of(code)
        here = region(name)
        slot = slot_of(packet(code))
        return pltpu.make_async_remote_copy(
            src_ref=here, dst_ref=here, send_sem=send_sem.at[slot], recv_sem=recv_sem.at[slot],
            device_id=neighbour(link), device_id_type=MESH)

    def receiving(name):
        here = region(name)
        slot = slot_of(name)
        return pltpu.make_async_remote_copy(
            src_ref=here, dst_ref=here, send_sem=send_sem.at[slot], recv_sem=recv_sem.at[slot],
            device_id=partner, device_id_type=MESH)

    def local(part):
        start, width = PARTS[part]
        return pltpu.make_async_copy(
            x_hbm.at[:, pl.ds(pl.multiple_of(q * FEATS + start, 128), width)],
            region((OWN, part, 0, 0)), load_sem.at[part])

    def swap(part):
        start, width = PARTS[part]
        return pltpu.make_async_remote_copy(
            src_ref=x_hbm.at[:, pl.ds(pl.multiple_of((1 - q) * FEATS + start, 128), width)],
            dst_ref=rows.at[q, y, z, :, pl.ds(start, width)],
            send_sem=x_send.at[part], recv_sem=x_recv.at[part], device_id=partner, device_id_type=MESH)

    def swapped(part):
        here = region((OTHER, part, 0, 0))
        return pltpu.make_async_remote_copy(
            src_ref=here, dst_ref=here, send_sem=x_send.at[part], recv_sem=x_recv.at[part],
            device_id=partner, device_id_type=MESH)

    pair, far = 3 * (y // 2), 3 * (1 - y // 2)
    tile_of = (pair + 2 * half, pair + 1, pair + 2 - 2 * half, far + 2 - 2 * half, far + 1, far + 2 * half)

    def exchange(k):
        return pltpu.make_async_remote_copy(
            src_ref=tiles.at[OTHER, tile_of[k]], dst_ref=arrived.at[tile_of[k]],
            send_sem=c_send.at[k], recv_sem=c_recv.at[k], device_id=partner, device_id_type=MESH)

    loads = (pltpu.make_async_copy(w_hbm, w, load_sem.at[2]),
             pltpu.make_async_copy(gate_hbm, gate, load_sem.at[3]),
             pltpu.make_async_copy(up_hbm, up, load_sem.at[4]))
    local(0).start()
    local(1).start()

    barrier = pltpu.get_barrier_semaphore()
    links = ((0, 1), (0, -1), (1, 1), (1, -1))
    for device in [neighbour(link) for link in links] + [partner]:
        pl.semaphore_signal(barrier, inc=1, device_id=device, device_id_type=MESH)
    pl.semaphore_wait(barrier, 5)
    swap(0).start()
    swap(1).start()
    for load in loads:
        load.start()

    actions, stage, waited, queue, block = [[]], [], set(), {link: [] for link in links}, 0
    for code in ORDER:
        if code >= 0:
            name, link = origin_of(code)
            if len(queue[link]) >= DEPTH:
                actions[-1].append(("sent", queue[link].pop(0)))
            if name not in waited:
                waited.add(name)
                actions[-1].append(("arrived", name))
            actions[-1].append(("send", code))
            queue[link].append(code)
        else:
            whose = OTHER if block < 4 else OWN
            for hy in NEEDS[block % 4]:
                for part in (0, 1):
                    for hz in Z_HOPS:
                        name = (whose, part, hy, hz)
                        if name not in waited:
                            waited.add(name)
                            actions[-1].append(("arrived", name))
            block += 1
            actions.append([])
    for action in actions.pop():
        actions[-1].append(action)
    left = [code for link in links for code in queue[link]]

    def act(kind, what):
        if kind == "send":
            sending(what).start()
        elif kind == "sent":
            sending(what).wait_send()
        elif what[2:] != (0, 0):
            receiving(what).wait_recv()
        elif what[0] == OWN:
            local(what[1]).wait()
        else:
            swapped(what[1]).wait_recv()

    def block_of(g, _):
        for b in range(8):
            @pl.when(g == b)
            def _():
                for kind, what in actions[b]:
                    act(kind, what)
                if b == 0:
                    loads[0].wait()
        whose = g // 4
        shard = (1 - whose) * (1 - q) + whose * q
        rank = g % 4
        is1, is2, is3 = rank * (2 - rank) * (3 - rank) // 2, rank * (rank - 1) * (3 - rank) // 2, rank * (rank - 1) * (rank - 2) // 6
        toward = 1 - 2 * half
        from_y = (y + is1 * toward - is2 * toward + is3 * 2 + NY) % NY
        acc[...] = jnp.zeros_like(acc)

        def step(i, _):
            k = pl.multiple_of(i * STEP, STEP)
            block = rows[shard, from_y, :, :, pl.ds(k, STEP)].astype(jnp.float32)
            block = block.reshape(NZ * ROWS, STEP).astype(jnp.bfloat16)
            acc[...] += lax.dot_general(
                w[:, pl.ds(k, STEP)], block, (((1,), (1,)), ((), ())), preferred_element_type=jnp.float32)
            return 0

        lax.fori_loop(0, FEATS // STEP, step, 0)
        first = 3 * (from_y // 2)

        @pl.when(from_y % 2 == 0)
        def _():
            tiles[whose, first] = acc[:, 0:128]
            tiles[whose, first + 1, :, 0:64] = acc[:, 128:192]

        @pl.when(from_y % 2 == 1)
        def _():
            tiles[whose, first + 1, :, 64:128] = acc[:, 0:64]
            tiles[whose, first + 2] = acc[:, 64:192]

        for b, ks in enumerate(((0,), (1, 2), (3,), (4, 5))):
            @pl.when(g == b)
            def _():
                for k in ks:
                    exchange(k).start()
        return 0

    lax.fori_loop(0, 8, block_of, 0)
    for code in left:
        sending(code).wait_send()
    loads[1].wait()
    loads[2].wait()

    live = live_ref[q]
    outs = []
    for k in range(6):
        exchange(k).wait_recv()
        tile = tile_of[k]
        lanes = pl.ds(pl.multiple_of(tile * 128, 128), 128)

        def finish(i, _):
            units = pl.ds(pl.multiple_of(i * 208, 16), 208)
            total = tiles[OWN, tile, units, :] + arrived[tile, units, :]
            row = tile * 128 + lax.broadcasted_iota(jnp.int32, total.shape, 1)
            total = jnp.where(row < live, total, 0.0)
            gate_value = gate[units, lanes].astype(jnp.float32)
            up_value = up[units, lanes].astype(jnp.float32)
            s = jax.nn.sigmoid(gate_value)
            out_u[k, units, :] = (total * gate_value * s).astype(jnp.bfloat16)
            out_g[k, units, :] = (total * up_value * s * (1.0 + gate_value * (1.0 - s))).astype(jnp.bfloat16)
            return 0

        lax.fori_loop(0, UNITS // 208, finish, 0)
        for n, (held, out) in enumerate(((out_g, gate_out), (out_u, up_out))):
            copy = pltpu.make_async_copy(held.at[k], out.at[:, lanes], out_sem.at[n, k])
            copy.start()
            outs.append(copy)
    swap(0).wait_send()
    swap(1).wait_send()
    for k in range(6):
        exchange(k).wait_send()
    for copy in outs:
        copy.wait()


def shards(grad_out, gate_pre, up_pre, down_weight, live_rows):
    anywhere = pl.BlockSpec(memory_space=pl.ANY)
    out = jax.ShapeDtypeStruct((UNITS, NY * NZ * ROWS), jnp.bfloat16)
    gate_grad, up_grad = pl.pallas_call(
        kernel,
        out_shape=(out, out),
        in_specs=[anywhere] * 4 + [pl.BlockSpec(memory_space=pltpu.SMEM)],
        out_specs=(anywhere, anywhere),
        scratch_shapes=[
            pltpu.VMEM((2, NY, NZ, ROWS, FEATS), jnp.bfloat16),
            pltpu.VMEM((UNITS, FEATS), jnp.bfloat16),
            pltpu.VMEM((UNITS, 768), jnp.bfloat16),
            pltpu.VMEM((UNITS, 768), jnp.bfloat16),
            pltpu.VMEM((UNITS, 192), jnp.float32),
            pltpu.VMEM((2, 6, UNITS, 128), jnp.float32),
            pltpu.VMEM((6, UNITS, 128), jnp.float32),
            pltpu.VMEM((6, UNITS, 128), jnp.bfloat16),
            pltpu.VMEM((6, UNITS, 128), jnp.bfloat16),
            pltpu.SemaphoreType.DMA((2, 2, 32)),
            pltpu.SemaphoreType.DMA((2, 2, 32)),
            pltpu.SemaphoreType.DMA((2,)),
            pltpu.SemaphoreType.DMA((2,)),
            pltpu.SemaphoreType.DMA((6,)),
            pltpu.SemaphoreType.DMA((6,)),
            pltpu.SemaphoreType.DMA((5,)),
            pltpu.SemaphoreType.DMA((2, 6)),
        ],
        compiler_params=pltpu.CompilerParams(
            collective_id=0, has_side_effects=True, vmem_limit_bytes=60 * 2**20),
        cost_estimate=pl.CostEstimate(flops=2 * 1536 * 832 * 4096, bytes_accessed=14 * 2**20, transcendentals=768 * 832),
    )(grad_out, down_weight, gate_pre.T, up_pre.T, live_rows)
    return gate_grad.T, up_grad.T


def solution(mesh):
    return jax.shard_map(
        shards,
        mesh=mesh,
        in_specs=(
            P(("section", "seq", "tensor"), None),
            P(("section", "seq"), "tensor"),
            P(("section", "seq"), "tensor"),
            P(("section", "tensor"), "seq"),
            P("section"),
        ),
        out_specs=(P(("section", "seq"), "tensor"), P(("section", "seq"), "tensor")),
        check_vma=False,
    )
```

```python
import functools

import jax
import jax.numpy as jnp
from jax import lax
from jax.experimental import pallas as pl
from jax.experimental.pallas import tpu as pltpu
from jax.sharding import PartitionSpec as P

MESH = pl.DeviceIdType.MESH
NY, NZ = 4, 8
ROWS, FEATS, UNITS = 24, 4096, 832
CUT = 2560
PARTS = ((0, CUT), (CUT, FEATS - CUT))
STEP = 1024
PIECE = 208
Y_HOPS = (0, 1, 2, -1)
Z_HOPS = (0, 1, 2, 3, 4, -1, -2, -3)
OTHER, OWN = 0, 1
ORDER = (
    104, 69, 97, 120, 101, 65, 88, 72, 8, 24, 1, 5, 112, 109, 121, 93, 40, 37, 33, 56, 77, 70, 66, 9, 29, 6, 2,
    25, 13, 45, 41, 89, 48, 61, 57, 90, 38, 34, 17, 7, 3, 10, 26, 46, 42, 14, 30, 62, 58, 39, 35, 21, 94, 53, 4,
    15, 31, 47, 43, 63, 11, 27, 59, 102, 36, 71, 22, 28, -1, -1, 49, 125, 44, 12, 54, 60, -1, 19, 103, 67, -1, 95,
    18, 110, 50, 126, -1, 23, -1, 55, 105, -1, 20, -1, 98, 16, 117, -1, 91, -1, 68, -1, 111, 74, -1, 51, 127, 85,
    75, 106, 118, -1, 78, -1, 122, 92, 79, 99, 113, 52, 119, 83, 107, 76, 123, 100, 73, 114, 87, -1, -1, 108, 82,
    -1, 124, -1, 84, -1, 115, -1, 81, -1, -1, 86, -1, -1, 80, -1, 116, -1, -1, -1, -2, -1, -1, -1, -1,
)
NEEDS = ((0,), (1, -1), (), (2,))
STEPS = FEATS // STEP


def packet(code):
    return (code // 64, code // 32 % 2, Y_HOPS[code // 8 % 4], Z_HOPS[code % 8])


def before(hops):
    return hops - 1 if hops > 0 else hops + 1


def origin_of(code):
    whose, part, hy, hz = packet(code)
    along_y = hy != 0 if part == 0 else hz == 0
    if along_y:
        return (whose, part, before(hy), hz), (0, 1 if hy > 0 else -1)
    return (whose, part, hy, before(hz)), (1, 1 if hz > 0 else -1)


def slot_of(name):
    whose, part, hy, hz = name
    return (part, whose, Y_HOPS.index(hy) * NZ + Z_HOPS.index(hz))


def kernel(x_hbm, w_hbm, gate_hbm, up_hbm, live_ref, gate_out, up_out,
           rows, w, gate, up, acc, tiles, coded, scale, coded_in, scale_in, out_g, out_u,
           send_sem, recv_sem, x_send, x_recv, c_send, c_recv, load_sem, out_sem):
    section, q, t = lax.axis_index("section"), lax.axis_index("seq"), lax.axis_index("tensor")
    y, z = t // NZ, t % NZ
    way = 1 - 2 * (section % 2)
    half = y % 2
    partner = (section, 1 - q, t)
    source = (q, 1 - q)

    def neighbour(link):
        axis, sign = link
        step = sign * way
        if axis == 0:
            return (section, q, (y + step + NY) % NY * NZ + z)
        return (section, q, y * NZ + (z + step + NZ) % NZ)

    def region(name):
        whose, part, hy, hz = name
        start, width = PARTS[part]
        shard = q if whose == OWN else 1 - q
        from_y = (y - way * hy + NY) % NY
        from_z = (z - way * hz + NZ) % NZ
        return rows.at[shard, from_y, from_z, :, pl.ds(start, width)]

    def sending(code):
        name, link = origin_of(code)
        here = region(name)
        slot = slot_of(packet(code))
        return pltpu.make_async_remote_copy(
            src_ref=here, dst_ref=here, send_sem=send_sem.at[slot], recv_sem=recv_sem.at[slot],
            device_id=neighbour(link), device_id_type=MESH)

    def receiving(name):
        here = region(name)
        slot = slot_of(name)
        return pltpu.make_async_remote_copy(
            src_ref=here, dst_ref=here, send_sem=send_sem.at[slot], recv_sem=recv_sem.at[slot],
            device_id=partner, device_id_type=MESH)

    def local(part):
        start, width = PARTS[part]
        return pltpu.make_async_copy(
            x_hbm.at[:, pl.ds(pl.multiple_of(q * FEATS + start, 128), width)],
            region((OWN, part, 0, 0)), load_sem.at[part])

    def swap(part):
        start, width = PARTS[part]
        return pltpu.make_async_remote_copy(
            src_ref=x_hbm.at[:, pl.ds(pl.multiple_of((1 - q) * FEATS + start, 128), width)],
            dst_ref=rows.at[q, y, z, :, pl.ds(start, width)],
            send_sem=x_send.at[part], recv_sem=x_recv.at[part], device_id=partner, device_id_type=MESH)

    def swapped(part):
        here = region((OTHER, part, 0, 0))
        return pltpu.make_async_remote_copy(
            src_ref=here, dst_ref=here, send_sem=x_send.at[part], recv_sem=x_recv.at[part],
            device_id=partner, device_id_type=MESH)

    pair, far = 3 * (y // 2), 3 * (1 - y // 2)
    tile_of = (pair + 2 * half, pair + 1, pair + 2 - 2 * half, far + 2 - 2 * half, far + 1, far + 2 * half)

    def exchange(k):
        def copy(n, src, dst):
            return pltpu.make_async_remote_copy(
                src_ref=src.at[k], dst_ref=dst.at[k], send_sem=c_send.at[n, k], recv_sem=c_recv.at[n, k],
                device_id=partner, device_id_type=MESH)

        return copy(0, scale, scale_in), copy(1, coded, coded_in)

    def encode(k):
        tile = tile_of[k]

        def some(i, _):
            units = pl.ds(pl.multiple_of(i * PIECE, 16), PIECE)
            part = tiles[OTHER, tile, units, :]
            row = tile * 128 + lax.broadcasted_iota(jnp.int32, part.shape, 1)
            part = jnp.where(row < live_ref[1 - q], part, 0.0)
            most = jnp.maximum(jnp.max(jnp.abs(part), axis=0, keepdims=True), 1e-30)
            coded[k, units, :] = jnp.round(part * (32767.0 / most)).astype(jnp.int32).astype(jnp.int16)
            scale[k, i] = jnp.broadcast_to(most * (1.0 / 32767.0), (8, 128))
            return 0

        lax.fori_loop(0, UNITS // PIECE, some, 0)

    loads = (pltpu.make_async_copy(w_hbm, w, load_sem.at[2]),
             pltpu.make_async_copy(gate_hbm, gate, load_sem.at[3]),
             pltpu.make_async_copy(up_hbm, up, load_sem.at[4]))
    local(0).start()
    local(1).start()

    barrier = pltpu.get_barrier_semaphore()
    links = ((0, 1), (0, -1), (1, 1), (1, -1))
    for device in [neighbour(link) for link in links] + [partner]:
        pl.semaphore_signal(barrier, inc=1, device_id=device, device_id_type=MESH)
    pl.semaphore_wait(barrier, 5)
    swap(0).start()
    swap(1).start()
    for load in loads:
        load.start()

    actions, waited, count = [[]], set(), 0

    def need(name):
        if name not in waited:
            waited.add(name)
            actions[-1].append(("arrived", name))

    for code in ORDER:
        if code >= 0:
            need(origin_of(code)[0])
            actions[-1].append(("send", code))
        elif code == -2:
            actions[-1].append(("finish", (0, 1, 2)))
        else:
            block, start = count // STEPS, count % STEPS * STEP
            for part in (0, 1):
                low, width = PARTS[part]
                if low < start + STEP and start < low + width:
                    for hy in NEEDS[block % 4]:
                        for hz in Z_HOPS:
                            need((OTHER if block < 4 else OWN, part, hy, hz))
            count += 1
            actions.append([])
    for action in actions.pop():
        actions[-1].append(action)

    def act(kind, what):
        if kind == "send":
            sending(what).start()
        elif kind == "finish":
            finish(what)
        elif what[2:] != (0, 0):
            receiving(what).wait_recv()
        elif what[0] == OWN:
            local(what[1]).wait()
        else:
            swapped(what[1]).wait_recv()

    live = live_ref[q]

    def result(n, k):
        lanes = pl.ds(pl.multiple_of(tile_of[k] * 128, 128), 128)
        return pltpu.make_async_copy(
            (out_g, out_u)[n].at[k], (gate_out, up_out)[n].at[:, lanes], out_sem.at[n, k])

    def finish(ks):
        if 0 in ks:
            loads[1].wait()
            loads[2].wait()
        for k in ks:
            for copy in exchange(k):
                copy.wait_recv()
            tile = tile_of[k]
            lanes = pl.ds(pl.multiple_of(tile * 128, 128), 128)

            def some(i, _):
                units = pl.ds(pl.multiple_of(i * PIECE, 16), PIECE)
                theirs = coded_in[k, units, :].astype(jnp.int32).astype(jnp.float32) * scale_in[k, i, 0:1, :]
                total = tiles[OWN, tile, units, :] + theirs
                row = tile * 128 + lax.broadcasted_iota(jnp.int32, total.shape, 1)
                total = jnp.where(row < live, total, 0.0)
                gate_value = gate[units, lanes].astype(jnp.float32)
                up_value = up[units, lanes].astype(jnp.float32)
                s = jax.nn.sigmoid(gate_value)
                out_u[k, units, :] = (total * gate_value * s).astype(jnp.bfloat16)
                out_g[k, units, :] = (total * up_value * s * (1.0 + gate_value * (1.0 - s))).astype(jnp.bfloat16)
                return 0

            lax.fori_loop(0, UNITS // PIECE, some, 0)
            result(0, k).start()
            result(1, k).start()

    def block_of(g, _):
        whose = g // 4
        shard = (1 - whose) * (1 - q) + whose * q
        rank = g % 4
        is1, is2, is3 = rank * (2 - rank) * (3 - rank) // 2, rank * (rank - 1) * (3 - rank) // 2, rank * (rank - 1) * (rank - 2) // 6
        toward = 1 - 2 * half
        from_y = (y + is1 * toward - is2 * toward + is3 * 2 + NY) % NY
        acc[...] = jnp.zeros_like(acc)

        def step(i, _):
            for b in range(8):
                @pl.when(g == b)
                def _():
                    for c in range(STEPS):
                        mine = actions[b * STEPS + c]
                        if mine or b + c == 0:
                            @pl.when(i == c)
                            def _():
                                for kind, what in mine:
                                    act(kind, what)
                                if b + c == 0:
                                    loads[0].wait()
            k = pl.multiple_of(i * STEP, STEP)
            block = rows[shard, from_y, :, :, pl.ds(k, STEP)].astype(jnp.float32)
            block = block.reshape(NZ * ROWS, STEP).astype(jnp.bfloat16)
            acc[...] += lax.dot_general(
                w[:, pl.ds(k, STEP)], block, (((1,), (1,)), ((), ())), preferred_element_type=jnp.float32)
            return 0

        lax.fori_loop(0, STEPS, step, 0)
        first = 3 * (from_y // 2)

        @pl.when(from_y % 2 == 0)
        def _():
            tiles[whose, first] = acc[:, 0:128]
            tiles[whose, first + 1, :, 0:64] = acc[:, 128:192]

        @pl.when(from_y % 2 == 1)
        def _():
            tiles[whose, first + 1, :, 64:128] = acc[:, 0:64]
            tiles[whose, first + 2] = acc[:, 64:192]

        for b, ks in enumerate(((0,), (1, 2), (3,), (4, 5))):
            @pl.when(g == b)
            def _():
                for k in ks:
                    encode(k)
                    for copy in exchange(k):
                        copy.start()
        return 0

    lax.fori_loop(0, 8, block_of, 0)
    finish((3, 4, 5) if -2 in ORDER else range(6))
    for code in ORDER:
        if code >= 0:
            sending(code).wait_send()
    for part in (0, 1):
        swap(part).wait_send()
    for k in range(6):
        for copy in exchange(k):
            copy.wait_send()
        result(0, k).wait()
        result(1, k).wait()


def shards(grad_out, gate_pre, up_pre, down_weight, live_rows):
    anywhere = pl.BlockSpec(memory_space=pl.ANY)
    out = jax.ShapeDtypeStruct((UNITS, NY * NZ * ROWS), jnp.bfloat16)
    gate_grad, up_grad = pl.pallas_call(
        kernel,
        out_shape=(out, out),
        in_specs=[anywhere] * 4 + [pl.BlockSpec(memory_space=pltpu.SMEM)],
        out_specs=(anywhere, anywhere),
        scratch_shapes=[
            pltpu.VMEM((2, NY, NZ, ROWS, FEATS), jnp.bfloat16),
            pltpu.VMEM((UNITS, FEATS), jnp.bfloat16),
            pltpu.VMEM((UNITS, 768), jnp.bfloat16),
            pltpu.VMEM((UNITS, 768), jnp.bfloat16),
            pltpu.VMEM((UNITS, 192), jnp.float32),
            pltpu.VMEM((2, 6, UNITS, 128), jnp.float32),
            pltpu.VMEM((6, UNITS, 128), jnp.int16),
            pltpu.VMEM((6, UNITS // PIECE, 8, 128), jnp.float32),
            pltpu.VMEM((6, UNITS, 128), jnp.int16),
            pltpu.VMEM((6, UNITS // PIECE, 8, 128), jnp.float32),
            pltpu.VMEM((6, UNITS, 128), jnp.bfloat16),
            pltpu.VMEM((6, UNITS, 128), jnp.bfloat16),
            pltpu.SemaphoreType.DMA((2, 2, 32)),
            pltpu.SemaphoreType.DMA((2, 2, 32)),
            pltpu.SemaphoreType.DMA((2,)),
            pltpu.SemaphoreType.DMA((2,)),
            pltpu.SemaphoreType.DMA((2, 6)),
            pltpu.SemaphoreType.DMA((2, 6)),
            pltpu.SemaphoreType.DMA((5,)),
            pltpu.SemaphoreType.DMA((2, 6)),
        ],
        compiler_params=pltpu.CompilerParams(
            collective_id=0, has_side_effects=True, vmem_limit_bytes=60 * 2**20),
        cost_estimate=pl.CostEstimate(flops=2 * 1536 * 832 * 4096, bytes_accessed=14 * 2**20, transcendentals=768 * 832),
    )(grad_out, down_weight, gate_pre.T, up_pre.T, live_rows)
    return gate_grad.T, up_grad.T


def solution(mesh):
    return jax.shard_map(
        shards,
        mesh=mesh,
        in_specs=(
            P(("section", "seq", "tensor"), None),
            P(("section", "seq"), "tensor"),
            P(("section", "seq"), "tensor"),
            P(("section", "tensor"), "seq"),
            P("section"),
        ),
        out_specs=(P(("section", "seq"), "tensor"), P(("section", "seq"), "tensor")),
        check_vma=False,
    )
```

```python
import functools

import jax
import jax.numpy as jnp
from jax import lax
from jax.experimental import pallas as pl
from jax.experimental.pallas import tpu as pltpu
from jax.sharding import PartitionSpec as P

MESH = pl.DeviceIdType.MESH
NY, NZ = 4, 8
ROWS, FEATS, UNITS = 24, 4096, 832
CUTS = (2560, 2432)
PARTS = tuple(((0, cut), (cut, FEATS - cut)) for cut in CUTS)
LAG = 24
PARCELS = 4
STEP = 2048
PIECE = 64
PIECES = UNITS // PIECE
Y_HOPS = (0, 1, 2, -1)
Z_HOPS = (0, 1, 2, 3, 4, -1, -2, -3)
OTHER, OWN = 0, 1
ORDER = (
    -4, -4, -4, -4, 65, 120, 101, 69, 72, 104, 97, 88, -4, -4, 1, 5, 8, 24, 121, 102, 73, 89, 33, 56, 37, 40, 66,
    125, 25, 13, 2, 6, 29, 9, 103, 34, 93, 48, 61, 41, 90, 45, 21, 57, 7, 10, 3, 30, 38, 35, 14, 26, 46, 42, 17,
    62, 58, 31, 53, 4, 11, 27, 39, 49, 47, 15, 59, 63, 22, 43, 54, 28, -1, 12, 36, 70, 50, 126, 19, 60, 23, 55,
    44, 18, 109, -1, 20, 51, 94, 67, 71, 80, -1, 127, 105, 16, -1, 110, 52, 77, 112, -1, 98, 78, 95, -1, 91, 68,
    74, -1, 106, 122, 111, 117, 79, -1, 113, 92, 99, 76, -1, 107, 75, 123, 118, 82, 114, 87, 100, 108, 84, 124,
    81, 119, 115, 85, -1, 83, -1, 86, -1, 116, -1, -1, -2, -1, -1,
)
NEEDS = ((0,), (1, -1), (), (2,))
STEPS = FEATS // STEP


def packet(code):
    return (code // 64, code // 32 % 2, Y_HOPS[code // 8 % 4], Z_HOPS[code % 8])


def before(hops):
    return hops - 1 if hops > 0 else hops + 1


def origin_of(code):
    whose, part, hy, hz = packet(code)
    along_y = hy != 0 if part == 0 else hz == 0
    if along_y:
        return (whose, part, before(hy), hz), (0, 1 if hy > 0 else -1)
    return (whose, part, hy, before(hz)), (1, 1 if hz > 0 else -1)


def slot_of(name):
    whose, part, hy, hz = name
    return (part, whose, Y_HOPS.index(hy) * NZ + Z_HOPS.index(hz))


def kernel(x_hbm, w_hbm, gate_hbm, up_hbm, live_ref, gate_out, up_out,
           rows, w, gate, up, acc, tiles, coded, scale, coded_in, scale_in, up_factor, gate_factor, out_g, out_u,
           send_sem, recv_sem, x_send, x_recv, c_send, c_recv, load_sem, out_sem):
    section, q, t = lax.axis_index("section"), lax.axis_index("seq"), lax.axis_index("tensor")
    y, z = t // NZ, t % NZ
    way = 1 - 2 * (section % 2)
    half = y % 2
    partner = (section, 1 - q, t)
    source = (q, 1 - q)

    def neighbour(link):
        axis, sign = link
        step = sign * way
        if axis == 0:
            return (section, q, (y + step + NY) % NY * NZ + z)
        return (section, q, y * NZ + (z + step + NZ) % NZ)

    def region(name):
        whose, part, hy, hz = name
        start, width = PARTS[whose][part]
        shard = q if whose == OWN else 1 - q
        from_y = (y - way * hy + NY) % NY
        from_z = (z - way * hz + NZ) % NZ
        return rows.at[shard, from_y, from_z, :, pl.ds(start, width)]

    def sending(code):
        name, link = origin_of(code)
        here = region(name)
        slot = slot_of(packet(code))
        return pltpu.make_async_remote_copy(
            src_ref=here, dst_ref=here, send_sem=send_sem.at[slot], recv_sem=recv_sem.at[slot],
            device_id=neighbour(link), device_id_type=MESH)

    def receiving(name):
        here = region(name)
        slot = slot_of(name)
        return pltpu.make_async_remote_copy(
            src_ref=here, dst_ref=here, send_sem=send_sem.at[slot], recv_sem=recv_sem.at[slot],
            device_id=partner, device_id_type=MESH)

    def local(part):
        start, width = PARTS[OWN][part]
        return pltpu.make_async_copy(
            x_hbm.at[:, pl.ds(pl.multiple_of(q * FEATS + start, 128), width)],
            region((OWN, part, 0, 0)), load_sem.at[part])

    def swap(part):
        start, width = PARTS[OTHER][part]
        return pltpu.make_async_remote_copy(
            src_ref=x_hbm.at[:, pl.ds(pl.multiple_of((1 - q) * FEATS + start, 128), width)],
            dst_ref=rows.at[q, y, z, :, pl.ds(start, width)],
            send_sem=x_send.at[part], recv_sem=x_recv.at[part], device_id=partner, device_id_type=MESH)

    def swapped(part):
        here = region((OTHER, part, 0, 0))
        return pltpu.make_async_remote_copy(
            src_ref=here, dst_ref=here, send_sem=x_send.at[part], recv_sem=x_recv.at[part],
            device_id=partner, device_id_type=MESH)

    pair, far = 3 * (y // 2), 3 * (1 - y // 2)
    tile_of = (pair + 2 * half, pair + 1, pair + 2 - 2 * half, far + 2 - 2 * half, far + 1, far + 2 * half)

    def exchange(k):
        def copy(n, src, dst):
            return pltpu.make_async_remote_copy(
                src_ref=src.at[k], dst_ref=dst.at[k], send_sem=c_send.at[n, k], recv_sem=c_recv.at[n, k],
                device_id=partner, device_id_type=MESH)

        return copy(0, scale, scale_in), copy(1, coded, coded_in)

    def encode(k):
        tile = tile_of[k]
        row = tile * 128 + lax.broadcasted_iota(jnp.int32, (PIECE, 128), 1)
        alive = row < live_ref[1 - q]
        scale[k, 8:16, :] = jnp.zeros((8, 128), jnp.float32)
        for i in range(PIECES):
            units = pl.ds(i * PIECE, PIECE)
            part = jnp.where(alive, tiles[OTHER, tile, units, :], 0.0)
            most = jnp.maximum(jnp.max(jnp.abs(part), axis=0, keepdims=True), 1e-30)
            coded[k, units, :] = jnp.round(part * (32767.0 / most)).astype(jnp.int32).astype(jnp.int16)
            scale[k, i:i + 1, :] = most * (1.0 / 32767.0)

    weights = pltpu.make_async_copy(w_hbm, w, load_sem.at[2])
    stored = (pltpu.make_async_copy(gate_hbm, gate, load_sem.at[3]),
              pltpu.make_async_copy(up_hbm, up, load_sem.at[4]))
    local(0).start()
    local(1).start()

    barrier = pltpu.get_barrier_semaphore()
    links = ((0, 1), (0, -1), (1, 1), (1, -1))
    for device in [neighbour(link) for link in links] + [partner]:
        pl.semaphore_signal(barrier, inc=1, device_id=device, device_id_type=MESH)
    pl.semaphore_wait(barrier, 5)
    swap(0).start()
    swap(1).start()
    for load in stored:
        load.start()
    weights.start()

    actions, waited, count, flying, factors = [[]], set(), 0, [], 0

    def need(name):
        if name not in waited:
            waited.add(name)
            actions[-1].append(("arrived", name))

    for code in ORDER:
        if code >= 0:
            need(origin_of(code)[0])
            actions[-1].append(("send", code))
            flying.append(code)
            if len(flying) > LAG:
                actions[-1].append(("sent", flying.pop(0)))
        elif code == -2:
            actions[-1].append(("finish", (0, 1, 2)))
        elif code == -4:
            actions[-1].append(("factor", factors))
            factors += 1
        else:
            block, start = count // STEPS, count % STEPS * STEP
            for part in (0, 1):
                low, width = PARTS[OTHER if block < 4 else OWN][part]
                if low < start + STEP and start < low + width:
                    for hy in NEEDS[block % 4]:
                        for hz in Z_HOPS:
                            need((OTHER if block < 4 else OWN, part, hy, hz))
            count += 1
            actions.append([])
    for action in actions.pop():
        actions[-1].append(action)

    def act(kind, what):
        if kind == "send":
            sending(what).start()
        elif kind == "sent":
            sending(what).wait_send()
        elif kind == "factor":
            factor(what)
        elif kind == "finish":
            finish(what)
        elif what[2:] != (0, 0):
            receiving(what).wait_recv()
        elif what[0] == OWN:
            local(what[1]).wait()
        else:
            swapped(what[1]).wait_recv()

    live = live_ref[q]

    def factor(n):
        if n == 0:
            for load in stored:
                load.wait()

        def some(i, _):
            units = pl.ds(pl.multiple_of(i * 208, 16), 208)
            gate_value = gate[units, n * 128:(n + 1) * 128].astype(jnp.float32)
            up_value = up[units, n * 128:(n + 1) * 128].astype(jnp.float32)
            s = jax.nn.sigmoid(gate_value)
            up_factor[n, units, :] = gate_value * s
            gate_factor[n, units, :] = up_value * s * (1.0 + gate_value * (1.0 - s))
            return 0

        lax.fori_loop(0, UNITS // 208, some, 0)

    def result(n, k):
        lanes = pl.ds(pl.multiple_of(tile_of[k] * 128, 128), 128)
        return pltpu.make_async_copy(
            (out_g, out_u)[n].at[k], (gate_out, up_out)[n].at[:, lanes], out_sem.at[n, k])

    def finish(ks):
        for k in ks:
            for copy in exchange(k):
                copy.wait_recv()
            tile = tile_of[k]
            row = tile * 128 + lax.broadcasted_iota(jnp.int32, (PIECE, 128), 1)
            alive = row < live
            for i in range(PIECES):
                units = pl.ds(i * PIECE, PIECE)
                theirs = coded_in[k, units, :].astype(jnp.int32).astype(jnp.float32) * scale_in[k, i:i + 1, :]
                sums = jnp.where(alive, tiles[OWN, tile, units, :] + theirs, 0.0)
                out_g[k, units, :] = (sums * gate_factor[tile, units, :]).astype(jnp.bfloat16)
                out_u[k, units, :] = (sums * up_factor[tile, units, :]).astype(jnp.bfloat16)
            result(0, k).start()
            result(1, k).start()

    def block_of(g, _):
        whose = g // 4
        shard = (1 - whose) * (1 - q) + whose * q
        rank = g % 4
        is1, is2, is3 = rank * (2 - rank) * (3 - rank) // 2, rank * (rank - 1) * (3 - rank) // 2, rank * (rank - 1) * (rank - 2) // 6
        toward = 1 - 2 * half
        from_y = (y + is1 * toward - is2 * toward + is3 * 2 + NY) % NY
        acc[...] = jnp.zeros_like(acc)

        def step(i, _):
            for b in range(8):
                @pl.when(g == b)
                def _():
                    for c in range(STEPS):
                        mine = actions[b * STEPS + c]
                        if mine or b + c == 0:
                            @pl.when(i == c)
                            def _():
                                for kind, what in mine:
                                    act(kind, what)
                                if b + c == 0:
                                    weights.wait()
            k = pl.multiple_of(i * STEP, STEP)
            block = rows[shard, from_y, :, :, pl.ds(k, STEP)].astype(jnp.float32)
            block = block.reshape(NZ * ROWS, STEP).astype(jnp.bfloat16)
            acc[...] += lax.dot_general(
                w[:, pl.ds(k, STEP)], block, (((1,), (1,)), ((), ())), preferred_element_type=jnp.float32)
            return 0

        lax.fori_loop(0, STEPS, step, 0)
        first = 3 * (from_y // 2)

        @pl.when(from_y % 2 == 0)
        def _():
            tiles[whose, first] = acc[:, 0:128]
            tiles[whose, first + 1, :, 0:64] = acc[:, 128:192]

        @pl.when(from_y % 2 == 1)
        def _():
            tiles[whose, first + 1, :, 64:128] = acc[:, 0:64]
            tiles[whose, first + 2] = acc[:, 64:192]

        for b, ks in enumerate(((0,), (1, 2), (3,), (4, 5))):
            @pl.when(g == b)
            def _():
                for k in ks:
                    encode(k)
                    for copy in exchange(k):
                        copy.start()
        return 0

    lax.fori_loop(0, 8, block_of, 0)
    finish((3, 4, 5) if -2 in ORDER else range(6))
    for code in flying:
        sending(code).wait_send()
    for part in (0, 1):
        swap(part).wait_send()
    for k in range(6):
        for copy in exchange(k):
            copy.wait_send()
        result(0, k).wait()
        result(1, k).wait()


def hand_over(gate_in, up_in, gate_out, up_out, held, in_sem, out_sem):
    loads, stores = [], []
    for i in range(PARCELS):
        units = pl.ds(i * (UNITS // PARCELS), UNITS // PARCELS)
        for n, (src, dst) in enumerate(((gate_in, gate_out), (up_in, up_out))):
            loads.append(pltpu.make_async_copy(src.at[units], held.at[n, units], in_sem.at[n, i]))
            stores.append(pltpu.make_async_copy(held.at[n, units], dst.at[units], out_sem.at[n, i]))
    for copy in loads:
        copy.start()
    for load, store in zip(loads, stores):
        load.wait()
        store.start()
    for copy in stores:
        copy.wait()


def shards(grad_out, gate_pre, up_pre, down_weight, live_rows):
    anywhere = pl.BlockSpec(memory_space=pl.ANY)
    out = jax.ShapeDtypeStruct((UNITS, NY * NZ * ROWS), jnp.bfloat16)
    tile_set = (6, UNITS, 128)
    gate_grad, up_grad = pl.pallas_call(
        kernel,
        out_shape=(out, out),
        in_specs=[anywhere] * 4 + [pl.BlockSpec(memory_space=pltpu.SMEM)],
        out_specs=(anywhere, anywhere),
        scratch_shapes=[
            pltpu.VMEM((2, NY, NZ, ROWS, FEATS), jnp.bfloat16),
            pltpu.VMEM((UNITS, FEATS), jnp.bfloat16),
            pltpu.VMEM((UNITS, NY * NZ * ROWS), jnp.bfloat16),
            pltpu.VMEM((UNITS, NY * NZ * ROWS), jnp.bfloat16),
            pltpu.VMEM((UNITS, 192), jnp.float32),
            pltpu.VMEM((2,) + tile_set, jnp.float32),
            pltpu.VMEM(tile_set, jnp.int16),
            pltpu.VMEM((6, 16, 128), jnp.float32),
            pltpu.VMEM(tile_set, jnp.int16),
            pltpu.VMEM((6, 16, 128), jnp.float32),
            pltpu.VMEM(tile_set, jnp.float32),
            pltpu.VMEM(tile_set, jnp.float32),
            pltpu.VMEM(tile_set, jnp.bfloat16),
            pltpu.VMEM(tile_set, jnp.bfloat16),
            pltpu.SemaphoreType.DMA((2, 2, 32)),
            pltpu.SemaphoreType.DMA((2, 2, 32)),
            pltpu.SemaphoreType.DMA((2,)),
            pltpu.SemaphoreType.DMA((2,)),
            pltpu.SemaphoreType.DMA((2, 6)),
            pltpu.SemaphoreType.DMA((2, 6)),
            pltpu.SemaphoreType.DMA((5,)),
            pltpu.SemaphoreType.DMA((2, 6)),
        ],
        compiler_params=pltpu.CompilerParams(
            collective_id=0, has_side_effects=True, vmem_limit_bytes=60 * 2**20),
        cost_estimate=pl.CostEstimate(flops=2 * 1536 * 832 * 4096, bytes_accessed=14 * 2**20, transcendentals=768 * 832),
    )(grad_out, down_weight, gate_pre.T, up_pre.T, live_rows)
    gate_grad, up_grad = pl.pallas_call(
        hand_over,
        out_shape=(out, out),
        in_specs=[anywhere] * 2,
        out_specs=(anywhere, anywhere),
        scratch_shapes=[
            pltpu.VMEM((2, UNITS, NY * NZ * ROWS), jnp.bfloat16),
            pltpu.SemaphoreType.DMA((2, PARCELS)),
            pltpu.SemaphoreType.DMA((2, PARCELS)),
        ],
        compiler_params=pltpu.CompilerParams(vmem_limit_bytes=60 * 2**20),
    )(gate_grad, up_grad)
    return gate_grad.T, up_grad.T


def solution(mesh):
    return jax.shard_map(
        shards,
        mesh=mesh,
        in_specs=(
            P(("section", "seq", "tensor"), None),
            P(("section", "seq"), "tensor"),
            P(("section", "seq"), "tensor"),
            P(("section", "tensor"), "seq"),
            P("section"),
        ),
        out_specs=(P(("section", "seq"), "tensor"), P(("section", "seq"), "tensor")),
        check_vma=False,
    )
```

```python
import functools

import jax
import jax.numpy as jnp
from jax import lax
from jax.experimental import pallas as pl
from jax.experimental.pallas import tpu as pltpu
from jax.sharding import PartitionSpec as P

MESH = pl.DeviceIdType.MESH
NY, NZ = 4, 8
ROWS, FEATS, UNITS = 24, 4096, 832
CUTS = (2560, 2432)
PARTS = tuple(((0, cut), (cut, FEATS - cut)) for cut in CUTS)
LAG = 24
PARCELS = 2
STEP = 2048
PIECE = 64
PIECES = UNITS // PIECE
Y_HOPS = (0, 1, 2, -1)
Z_HOPS = (0, 1, 2, 3, 4, -1, -2, -3)
OTHER, OWN = 0, 1
ORDER = (
    -4, -4, -4, -4, 65, 69, 101, 104, 120, 97, 72, 88, -4, -4, 1, 24, 5, 8, 105, 109, 112, 56, 33, 70, 40, 93, 66,
    37, 9, 25, 2, 13, 6, 29, 57, 45, 48, 94, 41, 61, 17, 34, 90, 38, 10, 3, 7, 26, 58, 14, 46, 30, 42, 21, 62, 35,
    53, 89, 18, 4, 39, 27, 59, 47, 11, 63, 31, 43, 15, 71, 49, -1, 28, 12, 36, 54, 60, 125, 19, 44, 110, 95, 67,
    102, 23, -1, 50, 55, 22, -1, 126, 20, 121, -1, 16, 103, 98, 91, 74, -1, 111, 51, -1, 127, 68, 77, 78, 117,
    106, -1, 73, 75, 99, 79, 122, 52, 86, 92, 118, 113, 76, 107, 100, 81, 123, -1, 114, 85, 80, 108, 119, -1, 87,
    124, -1, 115, 84, -1, 82, 83, -1, 116, -1, -1, -2, -1, -3, -1,
)
NEEDS = ((0,), (1, -1), (), (2,))
STEPS = FEATS // STEP


def packet(code):
    return (code // 64, code // 32 % 2, Y_HOPS[code // 8 % 4], Z_HOPS[code % 8])


def before(hops):
    return hops - 1 if hops > 0 else hops + 1


def origin_of(code):
    whose, part, hy, hz = packet(code)
    along_y = hy != 0 if part == 0 else hz == 0
    if along_y:
        return (whose, part, before(hy), hz), (0, 1 if hy > 0 else -1)
    return (whose, part, hy, before(hz)), (1, 1 if hz > 0 else -1)


def slot_of(name):
    whose, part, hy, hz = name
    return (part, whose, Y_HOPS.index(hy) * NZ + Z_HOPS.index(hz))


def kernel(x_hbm, w_hbm, gate_hbm, up_hbm, live_ref, gate_out, up_out,
           rows, w, gate, up, acc, tiles, coded, scale, coded_in, scale_in, up_factor, gate_factor, out_g, out_u,
           send_sem, recv_sem, x_send, x_recv, c_send, c_recv, load_sem, out_sem):
    section, q, t = lax.axis_index("section"), lax.axis_index("seq"), lax.axis_index("tensor")
    y, z = t // NZ, t % NZ
    way = 1 - 2 * (section % 2)
    half = y % 2
    partner = (section, 1 - q, t)
    source = (q, 1 - q)

    def neighbour(link):
        axis, sign = link
        step = sign * way
        if axis == 0:
            return (section, q, (y + step + NY) % NY * NZ + z)
        return (section, q, y * NZ + (z + step + NZ) % NZ)

    def region(name):
        whose, part, hy, hz = name
        start, width = PARTS[whose][part]
        shard = q if whose == OWN else 1 - q
        from_y = (y - way * hy + NY) % NY
        from_z = (z - way * hz + NZ) % NZ
        return rows.at[shard, from_y, from_z, :, pl.ds(start, width)]

    def sending(code):
        name, link = origin_of(code)
        here = region(name)
        slot = slot_of(packet(code))
        return pltpu.make_async_remote_copy(
            src_ref=here, dst_ref=here, send_sem=send_sem.at[slot], recv_sem=recv_sem.at[slot],
            device_id=neighbour(link), device_id_type=MESH)

    def receiving(name):
        here = region(name)
        slot = slot_of(name)
        return pltpu.make_async_remote_copy(
            src_ref=here, dst_ref=here, send_sem=send_sem.at[slot], recv_sem=recv_sem.at[slot],
            device_id=partner, device_id_type=MESH)

    def local(part):
        start, width = PARTS[OWN][part]
        return pltpu.make_async_copy(
            x_hbm.at[:, pl.ds(pl.multiple_of(q * FEATS + start, 128), width)],
            region((OWN, part, 0, 0)), load_sem.at[part])

    def swap(part):
        start, width = PARTS[OTHER][part]
        return pltpu.make_async_remote_copy(
            src_ref=x_hbm.at[:, pl.ds(pl.multiple_of((1 - q) * FEATS + start, 128), width)],
            dst_ref=rows.at[q, y, z, :, pl.ds(start, width)],
            send_sem=x_send.at[part], recv_sem=x_recv.at[part], device_id=partner, device_id_type=MESH)

    def swapped(part):
        here = region((OTHER, part, 0, 0))
        return pltpu.make_async_remote_copy(
            src_ref=here, dst_ref=here, send_sem=x_send.at[part], recv_sem=x_recv.at[part],
            device_id=partner, device_id_type=MESH)

    pair, far = 3 * (y // 2), 3 * (1 - y // 2)
    tile_of = (pair + 2 * half, pair + 1, pair + 2 - 2 * half, far + 2 - 2 * half, far + 1, far + 2 * half)

    def exchange(k):
        def copy(n, src, dst):
            return pltpu.make_async_remote_copy(
                src_ref=src.at[k], dst_ref=dst.at[k], send_sem=c_send.at[n, k], recv_sem=c_recv.at[n, k],
                device_id=partner, device_id_type=MESH)

        return copy(0, scale, scale_in), copy(1, coded, coded_in)

    def encode(k):
        tile = tile_of[k]
        row = tile * 128 + lax.broadcasted_iota(jnp.int32, (PIECE, 128), 1)
        alive = row < live_ref[1 - q]
        scale[k, 8:16, :] = jnp.zeros((8, 128), jnp.float32)
        for i in range(PIECES):
            units = pl.ds(i * PIECE, PIECE)
            part = jnp.where(alive, tiles[OTHER, tile, units, :], 0.0)
            most = jnp.maximum(jnp.max(jnp.abs(part), axis=0, keepdims=True), 1e-30)
            coded[k, units, :] = jnp.round(part * (32767.0 / most)).astype(jnp.int32).astype(jnp.int16)
            scale[k, i:i + 1, :] = most * (1.0 / 32767.0)

    weights = pltpu.make_async_copy(w_hbm, w, load_sem.at[2])
    stored = (pltpu.make_async_copy(gate_hbm, gate, load_sem.at[3]),
              pltpu.make_async_copy(up_hbm, up, load_sem.at[4]))
    local(0).start()
    local(1).start()

    barrier = pltpu.get_barrier_semaphore()
    links = ((0, 1), (0, -1), (1, 1), (1, -1))
    for device in [neighbour(link) for link in links] + [partner]:
        pl.semaphore_signal(barrier, inc=1, device_id=device, device_id_type=MESH)
    pl.semaphore_wait(barrier, 5)
    swap(0).start()
    swap(1).start()
    for load in stored:
        load.start()
    weights.start()

    actions, waited, count, flying, factors = [[]], set(), 0, [], 0

    def need(name):
        if name not in waited:
            waited.add(name)
            actions[-1].append(("arrived", name))

    for code in ORDER:
        if code >= 0:
            need(origin_of(code)[0])
            actions[-1].append(("send", code))
            flying.append(code)
            if len(flying) > LAG:
                actions[-1].append(("sent", flying.pop(0)))
        elif code == -2:
            actions[-1].append(("finish", (0, 1, 2)))
        elif code == -3:
            actions[-1].append(("finish", (3,)))
        elif code == -4:
            actions[-1].append(("factor", factors))
            factors += 1
        else:
            block, start = count // STEPS, count % STEPS * STEP
            for part in (0, 1):
                low, width = PARTS[OTHER if block < 4 else OWN][part]
                if low < start + STEP and start < low + width:
                    for hy in NEEDS[block % 4]:
                        for hz in Z_HOPS:
                            need((OTHER if block < 4 else OWN, part, hy, hz))
            count += 1
            actions.append([])
    for action in actions.pop():
        actions[-1].append(action)

    def act(kind, what):
        if kind == "send":
            sending(what).start()
        elif kind == "sent":
            sending(what).wait_send()
        elif kind == "factor":
            factor(what)
        elif kind == "finish":
            finish(what)
        elif what[2:] != (0, 0):
            receiving(what).wait_recv()
        elif what[0] == OWN:
            local(what[1]).wait()
        else:
            swapped(what[1]).wait_recv()

    live = live_ref[q]

    def factor(n):
        if n == 0:
            for load in stored:
                load.wait()

        def some(i, _):
            units = pl.ds(pl.multiple_of(i * 208, 16), 208)
            gate_value = gate[units, n * 128:(n + 1) * 128].astype(jnp.float32)
            up_value = up[units, n * 128:(n + 1) * 128].astype(jnp.float32)
            s = jax.nn.sigmoid(gate_value)
            up_factor[n, units, :] = gate_value * s
            gate_factor[n, units, :] = up_value * s * (1.0 + gate_value * (1.0 - s))
            return 0

        lax.fori_loop(0, UNITS // 208, some, 0)

    def result(n, k):
        lanes = pl.ds(pl.multiple_of(tile_of[k] * 128, 128), 128)
        return pltpu.make_async_copy(
            (out_g, out_u)[n].at[k], (gate_out, up_out)[n].at[:, lanes], out_sem.at[n, k])

    def finish(ks):
        for k in ks:
            for copy in exchange(k):
                copy.wait_recv()
            tile = tile_of[k]
            row = tile * 128 + lax.broadcasted_iota(jnp.int32, (PIECE, 128), 1)
            alive = row < live
            for i in range(PIECES):
                units = pl.ds(i * PIECE, PIECE)
                theirs = coded_in[k, units, :].astype(jnp.int32).astype(jnp.float32) * scale_in[k, i:i + 1, :]
                sums = jnp.where(alive, tiles[OWN, tile, units, :] + theirs, 0.0)
                out_g[k, units, :] = (sums * gate_factor[tile, units, :]).astype(jnp.bfloat16)
                out_u[k, units, :] = (sums * up_factor[tile, units, :]).astype(jnp.bfloat16)
            result(0, k).start()
            result(1, k).start()

    def block_of(g, _):
        whose = g // 4
        shard = (1 - whose) * (1 - q) + whose * q
        rank = g % 4
        is1, is2, is3 = rank * (2 - rank) * (3 - rank) // 2, rank * (rank - 1) * (3 - rank) // 2, rank * (rank - 1) * (rank - 2) // 6
        toward = 1 - 2 * half
        from_y = (y + is1 * toward - is2 * toward + is3 * 2 + NY) % NY
        acc[...] = jnp.zeros_like(acc)

        def step(i, _):
            for b in range(8):
                @pl.when(g == b)
                def _():
                    for c in range(STEPS):
                        mine = actions[b * STEPS + c]
                        if mine or b + c == 0:
                            @pl.when(i == c)
                            def _():
                                for kind, what in mine:
                                    act(kind, what)
                                if b + c == 0:
                                    weights.wait()
            k = pl.multiple_of(i * STEP, STEP)
            block = rows[shard, from_y, :, :, pl.ds(k, STEP)].astype(jnp.float32)
            block = block.reshape(NZ * ROWS, STEP).astype(jnp.bfloat16)
            acc[...] += lax.dot_general(
                w[:, pl.ds(k, STEP)], block, (((1,), (1,)), ((), ())), preferred_element_type=jnp.float32)
            return 0

        lax.fori_loop(0, STEPS, step, 0)
        first = 3 * (from_y // 2)

        @pl.when(from_y % 2 == 0)
        def _():
            tiles[whose, first] = acc[:, 0:128]
            tiles[whose, first + 1, :, 0:64] = acc[:, 128:192]

        @pl.when(from_y % 2 == 1)
        def _():
            tiles[whose, first + 1, :, 64:128] = acc[:, 0:64]
            tiles[whose, first + 2] = acc[:, 64:192]

        for b, ks in enumerate(((0,), (1, 2), (3,), (4, 5))):
            @pl.when(g == b)
            def _():
                for k in ks:
                    encode(k)
                    for copy in exchange(k):
                        copy.start()
        return 0

    lax.fori_loop(0, 8, block_of, 0)
    finish((4, 5))
    for code in flying:
        sending(code).wait_send()
    for part in (0, 1):
        swap(part).wait_send()
    for k in range(6):
        for copy in exchange(k):
            copy.wait_send()
        result(0, k).wait()
        result(1, k).wait()


def hand_over(gate_in, up_in, gate_out, up_out, sem):
    copies = []
    for n, (src, dst) in enumerate(((gate_in, gate_out), (up_in, up_out))):
        for i in range(PARCELS):
            units = pl.ds(i * (UNITS // PARCELS), UNITS // PARCELS)
            copies.append(pltpu.make_async_copy(src.at[units], dst.at[units], sem.at[n, i]))
    for copy in copies:
        copy.start()
    for copy in copies:
        copy.wait()


def shards(grad_out, gate_pre, up_pre, down_weight, live_rows):
    anywhere = pl.BlockSpec(memory_space=pl.ANY)
    out = jax.ShapeDtypeStruct((UNITS, NY * NZ * ROWS), jnp.bfloat16)
    tile_set = (6, UNITS, 128)
    gate_grad, up_grad = pl.pallas_call(
        kernel,
        out_shape=(pltpu.VMEM((UNITS, NY * NZ * ROWS), jnp.bfloat16),) * 2,
        in_specs=[pl.BlockSpec(memory_space=pltpu.HBM)] * 4 + [pl.BlockSpec(memory_space=pltpu.SMEM)],
        out_specs=(anywhere, anywhere),
        scratch_shapes=[
            pltpu.VMEM((2, NY, NZ, ROWS, FEATS), jnp.bfloat16),
            pltpu.VMEM((UNITS, FEATS), jnp.bfloat16),
            pltpu.VMEM((UNITS, NY * NZ * ROWS), jnp.bfloat16),
            pltpu.VMEM((UNITS, NY * NZ * ROWS), jnp.bfloat16),
            pltpu.VMEM((UNITS, 192), jnp.float32),
            pltpu.VMEM((2,) + tile_set, jnp.float32),
            pltpu.VMEM(tile_set, jnp.int16),
            pltpu.VMEM((6, 16, 128), jnp.float32),
            pltpu.VMEM(tile_set, jnp.int16),
            pltpu.VMEM((6, 16, 128), jnp.float32),
            pltpu.VMEM(tile_set, jnp.float32),
            pltpu.VMEM(tile_set, jnp.float32),
            pltpu.VMEM(tile_set, jnp.bfloat16),
            pltpu.VMEM(tile_set, jnp.bfloat16),
            pltpu.SemaphoreType.DMA((2, 2, 32)),
            pltpu.SemaphoreType.DMA((2, 2, 32)),
            pltpu.SemaphoreType.DMA((2,)),
            pltpu.SemaphoreType.DMA((2,)),
            pltpu.SemaphoreType.DMA((2, 6)),
            pltpu.SemaphoreType.DMA((2, 6)),
            pltpu.SemaphoreType.DMA((5,)),
            pltpu.SemaphoreType.DMA((2, 6)),
        ],
        compiler_params=pltpu.CompilerParams(
            collective_id=0, has_side_effects=True, vmem_limit_bytes=57 * 2**20),
        cost_estimate=pl.CostEstimate(flops=2 * 1536 * 832 * 4096, bytes_accessed=14 * 2**20, transcendentals=768 * 832),
    )(grad_out, down_weight, gate_pre.T, up_pre.T, live_rows)
    gate_grad, up_grad = pl.pallas_call(
        hand_over,
        out_shape=(out, out),
        in_specs=[anywhere] * 2,
        out_specs=(pl.BlockSpec(memory_space=pltpu.HBM),) * 2,
        scratch_shapes=[pltpu.SemaphoreType.DMA((2, PARCELS))],
        compiler_params=pltpu.CompilerParams(vmem_limit_bytes=2**20),
    )(gate_grad, up_grad)
    return gate_grad.T, up_grad.T


def solution(mesh):
    return jax.shard_map(
        shards,
        mesh=mesh,
        in_specs=(
            P(("section", "seq", "tensor"), None),
            P(("section", "seq"), "tensor"),
            P(("section", "seq"), "tensor"),
            P(("section", "tensor"), "seq"),
            P("section"),
        ),
        out_specs=(P(("section", "seq"), "tensor"), P(("section", "seq"), "tensor")),
        check_vma=False,
    )
```
